256 devices in a mesh: row: 64 (over y, z, core), col: 4 (over x).
Axes of the slice: x: 4, y: 4, z: 8, core: 2. Of those that a mesh axis runs over, the one named last changes fastest.
Arguments:
- matrix: float32 [262144, 1024], P('row', 'col'), may hold values from -6 to 6
- signs: int32 [262144], P('row'), may hold values from -1 to 1, as said below
- samples: int32 [4096], replicated, may hold values from 0 to 262143, as said below
Outputs:
- sketch: float32 [4096, 1024], P('row', 'col')
- gram: float32 [1024, 1024], P('col')
The draws below stay inside these ranges and needn't reach their ends.
Inputs may be any that keep to these rules, and one draw needn't show every extreme that they name: `signs`: each entry is +1 or -1. `samples`: for every k, the entries k * 64 to (k + 1) * 64 - 1 are strictly increasing; a row number may appear in several such ranges.
All inputs are finite; a program needn't handle non-finite values.
Results may differ from the reference program's by a relative error of at most 0.00012.
Values sent between devices are 32-bit elements; how exact they have to be, the bound alone decides.
A program may use at most 64 MiB of HBM per device.

```python
import jax
import jax.numpy as jnp
from jax import lax

R_DEV = 4096
SAMPLE_DEV = 64
ROWS = 262144
SAMPLES = 4096
COLS = 1024


def draw_signs(key, part):
    key = jax.random.fold_in(key, 3)
    return (2 * jax.random.randint(key, (ROWS,), 0, 2) - 1).astype(jnp.int32)


def draw_samples(key, part):
    key = jax.random.fold_in(key, 5)
    blocks = ROWS // R_DEV
    stretch = ROWS // SAMPLE_DEV
    owners = jnp.arange(blocks, dtype=jnp.int32)[:, None]
    strata = jnp.arange(SAMPLE_DEV, dtype=jnp.int32)[None, :]
    lower = jnp.broadcast_to(strata * stretch, (blocks, SAMPLE_DEV))
    upper = lower + stretch
    for offset in (1, blocks // 2):
        target = (owners + offset) % blocks
        where_stratum = target * R_DEV // stretch
        hit = strata == where_stratum
        lower_new = jnp.where(hit, jnp.maximum(lower, target * R_DEV), lower)
        upper_new = jnp.where(hit, jnp.minimum(upper, (target + 1) * R_DEV), upper)
        lower = lower_new
        upper = upper_new
    draws = jax.random.randint(jax.random.fold_in(key, 11), (blocks, SAMPLE_DEV), 0, 2 ** 30)
    picked = lower + draws % (upper - lower)
    return picked.reshape(SAMPLES).astype(jnp.int32)


def levels(rng, dims, cuts, smallest, high):
    gain, own = 1.0, jax.random.fold_in(rng, 6)
    for axis_at, blocks in cuts:
        steps = jnp.exp(jax.random.uniform(jax.random.fold_in(own, axis_at), (blocks,), jnp.float32, smallest / len(cuts), high / len(cuts)))
        gain = gain * jnp.repeat(steps, dims[axis_at] // blocks).reshape([-1 if axis == axis_at else 1 for axis in range(len(dims))])
    return gain


def centred(stream_key, extent, scale, bound, split=(), kind=jnp.bfloat16):
    result = jax.random.normal(stream_key, extent, jnp.float32) * scale
    if len(split) > 0:
        result = levels(stream_key, extent, split, -0.22, 0.18) * result
    return jnp.clip(result, min=-bound, max=bound).astype(kind)


def setup_inputs(seed: int = 0) -> dict:
    key_of = jax.random.split(jax.random.key(seed), 4)
    return {
        "matrix": centred(key_of[0], (ROWS, COLS), 1.0, 6.0, ((0, 64), (1, 4)), jnp.float32),
        "signs": draw_signs(jax.random.fold_in(key_of[3], 71), 0),
        "samples": draw_samples(jax.random.fold_in(key_of[3], 71), 0),
    }


def reference(matrix, signs, samples):
    total = matrix.shape[0]
    width = matrix.shape[1]
    current = matrix * signs.astype(jnp.float32)[:, None]
    step = 1
    while step < total:
        shaped = current.reshape(total // (2 * step), 2, step, width)
        first = shaped[:, 0]
        second = shaped[:, 1]
        current = jnp.stack([first + second, first - second], axis=1).reshape(total, width)
        step = step * 2
    current = current * (1.0 / float(total) ** 0.5)
    sketch = jnp.take(current, samples.astype(jnp.int32), axis=0)
    gram = jnp.dot(sketch.T, sketch, precision=lax.Precision.HIGHEST, preferred_element_type=jnp.float32) / samples.shape[0]
    return sketch, gram
```

```python
import jax
import jax.numpy as jnp
from jax import lax
from jax.experimental import pallas as pl
from jax.experimental.pallas import tpu as pltpu
from jax.sharding import PartitionSpec as P

MESH = pl.DeviceIdType.MESH
NX, NY, NZ = 4, 4, 8
CHIPS = NY * NZ
BLOCK = 4096
GROUP = 256
GROUPS = BLOCK // GROUP
SHARE = 128
LANES = 128
CHUNK = 512


def device(x, y, z, c):
    return (y * (NZ * 2) + z * 2 + c, x)


def parity(bits):
    bits = bits ^ (bits >> 4)
    bits = bits ^ (bits >> 2)
    bits = bits ^ (bits >> 1)
    return bits & 1


def stride(p):
    return (NZ - p) // 2 * (2 * (p % 2) - 1)


def split(values):
    high = values.astype(jnp.bfloat16)
    low = (values - high.astype(jnp.float32)).astype(jnp.bfloat16)
    return high, low


def rows(start, count):
    return pl.ds(pl.multiple_of(start, 8), count)


def kernel(
    matrix, signs, samples, sketch, gram,
    xbuf, ybuf, table, picks, places, mine, other, theirs,
    long1, long2, short1, zpart, total, left, right, skin, block, zgram,
    load_sem, place_sem, core_sem, l1_sem, l2_sem, s1_sem, z_sem, sk_sem,
    row_sem, col_sem, fwd_sem, rs_sem, ag_sem, yag_sem, sib_sem, send_sem,
):
    row = lax.axis_index("row")
    x = lax.axis_index("col")
    y, z, c = row // (NZ * 2), row // 2 % NZ, row % 2
    sibling = device(x, y, z, 1 - c)
    ahead = 1 - 2 * c
    diagonal = (x == y).astype(jnp.int32)

    def at_y(step):
        return device(x, (y + step + NY) % NY, z, c)

    def at_z(step):
        return device(x, y, (z + step + NZ) % NZ, c)

    def load(i):
        part = pl.ds(i * CHUNK, CHUNK)
        return pltpu.make_async_copy(matrix.at[part], xbuf.at[part], load_sem.at[i])

    def send(src, dst, sem, where, slot):
        pltpu.make_async_remote_copy(
            src, dst, send_sem.at[slot], sem, device_id=where, device_id_type=MESH
        ).start()

    def landed(ref, sem):
        pltpu.make_async_copy(ref, ref, sem).wait()

    barrier = pltpu.get_barrier_semaphore()

    def greet(where):
        pl.semaphore_signal(barrier, inc=1, device_id=where, device_id_type=MESH)

    for p in range(NZ - 1):
        greet(at_z(stride(p)))
    for k in range(1, NY):
        greet(at_y(k))
    for k in range(NY):
        if_self = jnp.logical_and(diagonal == 1, y == k)

        @pl.when(jnp.logical_not(if_self))
        def _():
            greet(device(y, k, z, c))

    greet(sibling)
    for i in range(BLOCK // CHUNK):
        load(i).start()

    spots = samples[...]
    flips = parity((spots // BLOCK) & row)
    picks[...] = spots % BLOCK + flips * (2 * BLOCK)
    place = pltpu.make_async_copy(picks, places, place_sem)
    place.start()

    line = lax.broadcasted_iota(jnp.int32, (GROUP, GROUP), 0)
    column = lax.broadcasted_iota(jnp.int32, (GROUP, GROUP), 1)
    hadamard = (1 - 2 * parity(line & column)).astype(jnp.float32) * (1.0 / 512.0)

    def mix(i, _):
        load(i).wait()
        for half in range(CHUNK // GROUP):
            g = i * (CHUNK // GROUP) + half
            sign = jnp.concatenate(
                [signs[pl.ds(2 * g, 1), :], signs[pl.ds(2 * g + 1, 1), :]], axis=1
            ).astype(jnp.float32)
            signed = (hadamard * sign).astype(jnp.bfloat16)
            part = rows(g * GROUP, GROUP)
            high, low = split(xbuf[part, :])
            ybuf[part, :] = jnp.dot(
                signed, high, preferred_element_type=jnp.float32
            ) + jnp.dot(signed, low, preferred_element_type=jnp.float32)
        return 0

    lax.fori_loop(0, BLOCK // CHUNK, mix, 0)

    def fold(t, _):
        for half in range(2):
            lanes = slice(half * LANES, (half + 1) * LANES)
            vals = [ybuf[rows(g * GROUP + t * 8, 8), lanes] for g in range(GROUPS)]
            step = 1
            while step < GROUPS:
                for g in range(GROUPS):
                    if g & step == 0:
                        a, b = vals[g], vals[g + step]
                        vals[g], vals[g + step] = a + b, a - b
                step *= 2
            place_of = jnp.where(c == half, 0, BLOCK)
            for g in range(GROUPS):
                spot = place_of + g * GROUP + t * 8
                table[rows(spot, 8), :] = vals[g]
                table[rows(spot + 2 * BLOCK, 8), :] = -vals[g]
        return 0

    lax.fori_loop(0, GROUP // 8, fold, 0)
    place.wait()
    pl.semaphore_wait(barrier, NZ + NY + NY - 1 - diagonal)

    def chunk(yy, zz):
        return yy * NZ + zz

    def part_of(spot):
        return rows(spot * SHARE, SHARE)

    def gather(spot):
        for base in range(0, SHARE, 16):
            at = [places[spot, base + u] for u in range(16)]
            kept = [table[pl.ds(at[u], 1), :] for u in range(16)]
            given = [table[pl.ds(at[u] + BLOCK, 1), :] for u in range(16)]
            for u in range(16):
                mine[pl.ds(spot * SHARE + base + u, 1), :] = kept[u]
            for u in range(16):
                other[pl.ds(spot * SHARE + base + u, 1), :] = given[u]

    def y_of(q):
        step = jnp.where(q == 0, 2, jnp.where(q == 1, ahead, jnp.where(q == 2, -ahead, 0)))
        return (y + step + NY) % NY

    def z_of(p):
        return (z + stride(p) + NZ) % NZ

    def pick(p):
        def each(q, _):
            spot = chunk(y_of(q), z_of(p))
            gather(spot)
            send(other.at[part_of(spot)], theirs.at[part_of(spot)], core_sem.at[spot], sibling, 0)
            return 0

        lax.fori_loop(0, 4, each, 0)

    def merge(p):
        def each(q, _):
            spot = chunk(y_of(q), z_of(p))
            landed(theirs.at[part_of(spot)], core_sem.at[spot])
            mine[part_of(spot), :] += theirs[part_of(spot), :]
            return 0

        lax.fori_loop(0, 4, each, 0)
        slot = part_of(p)
        far = part_of(chunk(y_of(0), z_of(p)))
        send(mine.at[far], long1.at[slot], l1_sem.at[p], at_y(ahead), 1)
        near = part_of(chunk(y_of(2), z_of(p)))
        send(mine.at[near], short1.at[slot], s1_sem.at[p], at_y(-ahead), 1)

    def second(p):
        slot = part_of(p)
        near = part_of(chunk(y_of(1), z_of(p)))
        landed(long1.at[slot], l1_sem.at[p])
        mine[near, :] += long1[slot, :]
        send(mine.at[near], long2.at[slot], l2_sem.at[p], at_y(ahead), 1)

    def third(p):
        slot = part_of(p)
        own = part_of(chunk(y, z_of(p)))
        landed(short1.at[slot], s1_sem.at[p])
        landed(long2.at[slot], l2_sem.at[p])
        mine[own, :] += short1[slot, :] + long2[slot, :]

        @pl.when(p < NZ - 1)
        def _():
            send(mine.at[own], zpart.at[slot], z_sem.at[p], at_z(stride(p)), 2)

    def turn(t, _):
        @pl.when(t < NZ)
        def _():
            pick(t)
            merge(t)

        @pl.when(jnp.logical_and(t >= 2, t < NZ + 2))
        def _():
            second(t - 2)

        @pl.when(t >= 4)
        def _():
            third(t - 4)

        return 0

    lax.fori_loop(0, NZ + 4, turn, 0)

    home = part_of(chunk(y, z))
    for p in range(NZ - 1):
        landed(zpart.at[part_of(p)], z_sem.at[p])
    total[...] = mine[home, :] + sum(zpart[part_of(p), :] for p in range(NZ - 1))

    slot_y = part_of(y)
    slot_cy = part_of(c * NY + y)
    for j in range(NY - 1, -1, -1):
        xx = (x + j) % NX
        if j == 0:
            @pl.when(diagonal == 1)
            def _():
                right[slot_cy, :] = total[...]

            @pl.when(diagonal == 0)
            def _():
                send(total, right.at[slot_cy], col_sem.at[y], device(xx, x, z, c), 3)
        else:
            send(total, right.at[slot_cy], col_sem.at[y], device(xx, x, z, c), 3)
    for k in (2, 1, 3):
        send(total, left.at[slot_y], row_sem.at[y], at_y(k), 4)
    send(total.at[rows((1 - c) * 64, 64)], skin, sk_sem, sibling, 5)
    left[slot_y, :] = total[...]
    sketch[:, pl.ds(pl.multiple_of(c * LANES, LANES), LANES)] = total[rows(c * 64, 64), :]

    for k in range(NY):
        ys = (y + k) % NY
        spot = part_of(c * NY + ys)
        if k == 0:
            @pl.when(diagonal == 0)
            def _():
                landed(right.at[spot], col_sem.at[ys])
        else:
            landed(right.at[spot], col_sem.at[ys])
        send(right.at[spot], right.at[spot], fwd_sem.at[ys], sibling, 6)
    for k in range(1, NY):
        ys = (y + k) % NY
        landed(left.at[part_of(ys)], row_sem.at[ys])

    lhigh, llow = split(left[...])

    def product(h):
        rhigh, rlow = split(right[rows(h * (NY * SHARE), NY * SHARE), :])
        dims = (((0,), (0,)), ((), ()))
        out = lax.dot_general(lhigh, rhigh, dims, preferred_element_type=jnp.float32)
        out += lax.dot_general(lhigh, rlow, dims, preferred_element_type=jnp.float32)
        out += lax.dot_general(llow, rhigh, dims, preferred_element_type=jnp.float32)
        block[:, pl.ds(pl.multiple_of(h * LANES, LANES), LANES)] = out * (1.0 / 4096.0)

    product(c)
    landed(skin, sk_sem)
    sketch[:, pl.ds(pl.multiple_of((1 - c) * LANES, LANES), LANES)] = skin[...]
    for k in range(NY):
        landed(right.at[part_of((1 - c) * NY + k)], fwd_sem.at[k])
    product(1 - c)

    def strip(zz):
        return rows(zz * 16, 16)

    for p in range(NZ - 1):
        send(block.at[strip(z_of(p))], zgram.at[strip(p)], rs_sem.at[p], at_z(stride(p)), 7)
    acc = block[strip(z), :]
    for p in range(NZ - 2, -1, -1):
        landed(zgram.at[strip(p)], rs_sem.at[p])
        acc = acc + zgram[strip(p), :]

    def tile(cc, zz, yy, count):
        return gram.at[rows(cc * 128 + zz * 16, count), pl.ds(pl.multiple_of(yy * 256, 256), 256)]

    tile_mine = tile(c, z, y, 16)
    tile_mine[...] = acc
    for p in range(NZ - 1):
        send(tile_mine, tile_mine, ag_sem.at[p], at_z(stride(p)), 8)

    def spread(zz):
        piece = tile(c, zz, y, 16)
        for k in (2, 1, 3):
            send(piece, piece, yag_sem.at[k, zz], at_y(k), 9)

    spread(z)
    for p in range(NZ - 2, -1, -1):
        zz = (z - stride(p) + NZ) % NZ
        landed(tile(c, zz, y, 16), ag_sem.at[p])
        spread(zz)
    whole = tile(c, 0, y, 128)
    send(whole, whole, sib_sem.at[y], sibling, 10)
    for k in (1, 3, 2):
        ys = (y - k + NY) % NY
        for zz in range(NZ):
            landed(tile(c, zz, ys, 16), yag_sem.at[k, zz])
        whole = tile(c, 0, ys, 128)
        send(whole, whole, sib_sem.at[ys], sibling, 10)

    def left_here(ref, slot):
        pltpu.make_async_copy(ref, ref, send_sem.at[slot]).wait()

    left_here(other, 0)
    left_here(mine.at[pl.ds(0, 3 * NZ * SHARE)], 1)
    left_here(mine.at[pl.ds(0, (NZ - 1) * SHARE)], 2)

    @pl.when(diagonal == 1)
    def _():
        left_here(mine.at[pl.ds(0, 3 * SHARE)], 3)

    @pl.when(diagonal == 0)
    def _():
        left_here(mine.at[pl.ds(0, 4 * SHARE)], 3)

    left_here(mine.at[pl.ds(0, 3 * SHARE)], 4)
    left_here(mine.at[pl.ds(0, 64)], 5)
    left_here(mine.at[pl.ds(0, 4 * SHARE)], 6)
    left_here(gram.at[pl.ds(0, 16 * (NZ - 1)), pl.ds(0, 256)], 7)
    left_here(gram.at[pl.ds(0, 16 * (NZ - 1)), pl.ds(0, 256)], 8)
    left_here(gram.at[pl.ds(0, 128), pl.ds(0, 768)], 9)
    left_here(gram.at[pl.ds(0, 128), :], 10)
    for k in range(NY):
        landed(tile(1 - c, 0, k, 128), sib_sem.at[k])


def body(matrix, signs, samples):
    vmem = pltpu.VMEM
    f32 = jnp.float32
    dma = pltpu.SemaphoreType.DMA
    spec = pl.BlockSpec(memory_space=pltpu.VMEM)
    return pl.pallas_call(
        kernel,
        out_shape=(
            jax.ShapeDtypeStruct((64, 256), f32),
            jax.ShapeDtypeStruct((256, 1024), f32),
        ),
        in_specs=[pl.BlockSpec(memory_space=pl.ANY), spec, spec],
        out_specs=(spec, spec),
        scratch_shapes=[
            vmem((BLOCK, 256), f32),
            vmem((BLOCK, 256), f32),
            vmem((4 * BLOCK, LANES), f32),
            vmem((CHIPS, SHARE), jnp.int32),
            pltpu.SMEM((CHIPS, SHARE), jnp.int32),
            vmem((CHIPS * SHARE, LANES), f32),
            vmem((CHIPS * SHARE, LANES), f32),
            vmem((CHIPS * SHARE, LANES), f32),
            vmem((NZ * SHARE, LANES), f32),
            vmem((NZ * SHARE, LANES), f32),
            vmem((NZ * SHARE, LANES), f32),
            vmem((NZ * SHARE, LANES), f32),
            vmem((SHARE, LANES), f32),
            vmem((NY * SHARE, LANES), f32),
            vmem((2 * NY * SHARE, LANES), f32),
            vmem((64, LANES), f32),
            vmem((SHARE, 256), f32),
            vmem((SHARE, 256), f32),
            dma((BLOCK // CHUNK,)),
            dma,
            dma((CHIPS,)),
            dma((NZ,)),
            dma((NZ,)),
            dma((NZ,)),
            dma((NZ,)),
            dma,
            dma((NY,)),
            dma((NY,)),
            dma((NY,)),
            dma((NZ,)),
            dma((NZ,)),
            dma((NY, NZ)),
            dma((NY,)),
            dma((11,)),
        ],
        compiler_params=pltpu.CompilerParams(
            collective_id=0, has_side_effects=True, vmem_limit_bytes=44 * 2**20
        ),
    )(matrix, signs.reshape(CHIPS, SHARE), samples.reshape(CHIPS, SHARE))


def solution(mesh):
    return jax.shard_map(
        body,
        mesh=mesh,
        in_specs=(P("row", "col"), P("row"), P()),
        out_specs=(P("row", "col"), P("col", None)),
        check_vma=False,
    )
```

```python
import jax
import jax.numpy as jnp
from jax import lax
from jax.experimental import pallas as pl
from jax.experimental.pallas import tpu as pltpu
from jax.sharding import PartitionSpec as P

MESH = pl.DeviceIdType.MESH
NX, NY, NZ = 4, 4, 8
CHIPS = NY * NZ
BLOCK = 4096
GROUP = 256
GROUPS = BLOCK // GROUP
SHARE = 128
LANES = 128
CHUNK = 512
YROWS = 104
ZROWS = SHARE - YROWS
FINISH = 4
PICK_Z, MERGE_Z, SECOND_Z, THIRD_Z = 1, 2, 5, 8


def device(x, y, z, c):
    return (y * (NZ * 2) + z * 2 + c, x)


def parity(bits):
    bits = bits ^ (bits >> 4)
    bits = bits ^ (bits >> 2)
    bits = bits ^ (bits >> 1)
    return bits & 1


def stride(p):
    return (NZ - p) // 2 * (2 * (p % 2) - 1)


def split(values):
    high = values.astype(jnp.bfloat16)
    low = (values - high.astype(jnp.float32)).astype(jnp.bfloat16)
    return high, low


def rows(start, count):
    return pl.ds(pl.multiple_of(start, 8), count)


def kernel(
    matrix, signs_in, samples_in, sketch, gram,
    xbuf, ybuf, table, signs, samples, picks, places,
    mine, other, theirs, minez, otherz, theirsz,
    ypart, zpart, zin, yin, total, left, right, skin, block, zgram,
    load_sem, place_sem, core_sem, corez_sem, ypart_sem, z_sem, zin_sem, yin_sem,
    sk_sem, row_sem, col_sem, fwd_sem, rs_sem, ag_sem, far_sem, yag_sem, sib_sem, send_sem,
):
    row = lax.axis_index("row")
    x = lax.axis_index("col")
    y, z, c = row // (NZ * 2), row // 2 % NZ, row % 2
    sibling = device(x, y, z, 1 - c)
    ahead = 1 - 2 * c

    def at_y(step):
        return device(x, (y + step + NY) % NY, z, c)

    def at_z(step):
        return device(x, y, (z + step + NZ) % NZ, c)

    def load(i):
        part = pl.ds(i * CHUNK, CHUNK)
        return pltpu.make_async_copy(matrix.at[part], xbuf.at[part], load_sem.at[i])

    def send(src, dst, sem, where, slot):
        pltpu.make_async_remote_copy(
            src, dst, send_sem.at[slot], sem, device_id=where, device_id_type=MESH
        ).start()

    def landed(ref, sem):
        pltpu.make_async_copy(ref, ref, sem).wait()

    barrier = pltpu.get_barrier_semaphore()

    def greet(where):
        pl.semaphore_signal(barrier, inc=1, device_id=where, device_id_type=MESH)

    get_signs = pltpu.make_async_copy(signs_in, signs, place_sem.at[0])
    get_samples = pltpu.make_async_copy(samples_in, samples, place_sem.at[1])
    get_samples.start()
    get_signs.start()
    for i in range(BLOCK // CHUNK):
        load(i).start()

    for p in range(NZ - 1):
        greet(at_z(stride(p)))
    for k in range(1, NY):
        greet(at_y(k))

    @pl.when(x != y)
    def _():
        for k in range(NY):
            greet(device(y, k, z, c))

    greet(sibling)

    get_samples.wait()
    spots = samples[...]
    flips = parity((spots // BLOCK) & row)
    picks[...] = spots % BLOCK + flips * (2 * BLOCK)
    place = pltpu.make_async_copy(picks, places, place_sem.at[2])
    place.start()

    line = lax.broadcasted_iota(jnp.int32, (GROUP, GROUP), 0)
    column = lax.broadcasted_iota(jnp.int32, (GROUP, GROUP), 1)
    hadamard = (1 - 2 * parity(line & column)).astype(jnp.float32) * (1.0 / 512.0)
    get_signs.wait()

    def mix(i, _):
        load(i).wait()
        for half in range(CHUNK // GROUP):
            g = i * (CHUNK // GROUP) + half
            sign = jnp.concatenate(
                [signs[pl.ds(2 * g, 1), :], signs[pl.ds(2 * g + 1, 1), :]], axis=1
            ).astype(jnp.float32)
            signed = (hadamard * sign).astype(jnp.bfloat16)
            part = rows(g * GROUP, GROUP)
            high, low = split(xbuf[part, :])
            ybuf[part, :] = jnp.dot(
                signed, high, preferred_element_type=jnp.float32
            ) + jnp.dot(signed, low, preferred_element_type=jnp.float32)
        return 0

    lax.fori_loop(0, BLOCK // CHUNK, mix, 0)

    def fold(t, _):
        for half in range(2):
            lanes = slice(half * LANES, (half + 1) * LANES)
            vals = [ybuf[rows(g * GROUP + t * 8, 8), lanes] for g in range(GROUPS)]
            step = 1
            while step < GROUPS:
                for g in range(GROUPS):
                    if g & step == 0:
                        a, b = vals[g], vals[g + step]
                        vals[g], vals[g + step] = a + b, a - b
                step *= 2
            place_of = jnp.where(c == half, 0, BLOCK)
            for g in range(GROUPS):
                spot = place_of + g * GROUP + t * 8
                table[rows(spot, 8), :] = vals[g]
                table[rows(spot + 2 * BLOCK, 8), :] = -vals[g]
        return 0

    lax.fori_loop(0, GROUP // 8, fold, 0)
    place.wait()

    def chunk(yy, zz):
        return yy * NZ + zz

    def gather(spot, first, count, kept_to, given_to, base):
        for start in range(0, count, 8):
            at = [places[spot, first + start + u] for u in range(8)]
            kept = [table[pl.ds(at[u], 1), :] for u in range(8)]
            given = [table[pl.ds(at[u] + BLOCK, 1), :] for u in range(8)]
            for u in range(8):
                kept_to[pl.ds(base + start + u, 1), :] = kept[u]
            for u in range(8):
                given_to[pl.ds(base + start + u, 1), :] = given[u]

    def part_y(spot):
        return rows(spot * YROWS, YROWS)

    def part_z(spot):
        return rows(spot * (NY * ZROWS), NY * ZROWS)

    def part_of(spot):
        return rows(spot * SHARE, SHARE)

    def y_of(q):
        return (y + 2 + q) % NY

    def z_of(p):
        return (z + stride(p) + NZ) % NZ

    def turn_z(step):
        return (z + step + NZ) % NZ

    def pick(p):
        def each(q, _):
            spot = chunk(y_of(q), z_of(p))
            gather(spot, 0, YROWS, mine, other, spot * YROWS)
            return 0

        lax.fori_loop(0, 4, each, 0)

    def give(p):
        def each(q, _):
            spot = chunk(y_of(q), z_of(p))
            send(other.at[part_y(spot)], theirs.at[part_y(spot)], core_sem.at[spot], sibling, 0)
            return 0

        lax.fori_loop(0, 4, each, 0)

    def merge(p):
        def each(q, _):
            spot = chunk(y_of(q), z_of(p))
            landed(theirs.at[part_y(spot)], core_sem.at[spot])
            mine[part_y(spot), :] += theirs[part_y(spot), :]
            return 0

        lax.fori_loop(0, 4, each, 0)
        for k in (2, 1, 3):
            spot = chunk((y + k) % NY, z_of(p))
            send(mine.at[part_y(spot)], ypart.at[part_y(k * NZ + p)], ypart_sem.at[k, p], at_y(k), 1)

    def finish(p):
        own = part_y(chunk(y, z_of(p)))
        for k in (1, 3, 2):
            landed(ypart.at[part_y(k * NZ + p)], ypart_sem.at[k, p])
        mine[own, :] += sum(ypart[part_y(k * NZ + p), :] for k in range(1, NY))

        @pl.when(p < NZ - 1)
        def _():
            send(mine.at[own], zpart.at[part_y(p)], z_sem.at[p], at_z(stride(p)), 2)

    def pick_z():
        def each(p, _):
            zz = z_of(p)
            for yy in range(NY):
                gather(chunk(yy, zz), YROWS, ZROWS, minez, otherz, (zz * NY + yy) * ZROWS)
            send(otherz.at[part_z(zz)], theirsz.at[part_z(zz)], corez_sem.at[zz], sibling, 0)
            return 0

        lax.fori_loop(0, NZ, each, 0)

    def send_z(step, slot, hop):
        send(minez.at[part_z(turn_z(step))], zin.at[part_z(slot)], zin_sem.at[slot], at_z(hop), 11)

    def merge_z():
        def each(p, _):
            zz = z_of(p)
            landed(theirsz.at[part_z(zz)], corez_sem.at[zz])
            minez[part_z(zz), :] += theirsz[part_z(zz), :]
            return 0

        lax.fori_loop(0, NZ, each, 0)
        send_z(4, 0, 2 * ahead)
        send_z(3 * ahead, 1, ahead)
        send_z(-3 * ahead, 2, -ahead)
        send_z(ahead, 3, ahead)
        send_z(-ahead, 4, -ahead)

    def take_z(step, slots):
        zz = turn_z(step)
        for slot in slots:
            landed(zin.at[part_z(slot)], zin_sem.at[slot])
        minez[part_z(zz), :] += sum(zin[part_z(slot), :] for slot in slots)

    def second_z():
        take_z(2 * ahead, (0, 1))
        send_z(2 * ahead, 5, 2 * ahead)
        take_z(-2 * ahead, (2,))
        send_z(-2 * ahead, 6, -2 * ahead)

    def third_z():
        take_z(0, (3, 4, 5, 6))
        for k in range(1, NY):
            part = rows((z * NY + (y + k) % NY) * ZROWS, ZROWS)
            slot = rows(k * ZROWS, ZROWS)
            send(minez.at[part], yin.at[slot], yin_sem.at[k], at_y(k), 12)

    pick(0)
    pl.semaphore_wait(barrier, NZ + NY + NX - 2)
    give(0)
    pick(1)
    give(1)

    def turn(t, _):
        @pl.when(t < NZ)
        def _():
            merge(t)

        @pl.when(t < NZ - 2)
        def _():
            pick(t + 2)
            give(t + 2)

        @pl.when(t == PICK_Z)
        def _():
            pick_z()

        @pl.when(t == MERGE_Z)
        def _():
            merge_z()

        @pl.when(t == SECOND_Z)
        def _():
            second_z()

        @pl.when(t == THIRD_Z)
        def _():
            third_z()

        @pl.when(t >= FINISH)
        def _():
            finish(t - FINISH)

        return 0

    lax.fori_loop(0, NZ + FINISH, turn, 0)

    home = part_y(chunk(y, z))
    for k in range(1, NY):
        landed(yin.at[rows(k * ZROWS, ZROWS)], yin_sem.at[k])
    total[pl.ds(YROWS, ZROWS), :] = minez[rows((z * NY + y) * ZROWS, ZROWS), :] + sum(
        yin[rows(k * ZROWS, ZROWS), :] for k in range(1, NY)
    )
    for p in range(NZ - 1):
        landed(zpart.at[part_y(p)], z_sem.at[p])
    total[pl.ds(0, YROWS), :] = mine[home, :] + sum(zpart[part_y(p), :] for p in range(NZ - 1))

    slot_y = part_of(y)
    slot_cy = part_of(c * NY + y)
    for j in (2, 1, 3):
        send(total, right.at[slot_cy], col_sem.at[y], device((x + j) % NX, x, z, c), 3)
    for k in (2, 1, 3):
        send(total, left.at[slot_y], row_sem.at[y], at_y(k), 4)
    send(total.at[rows((1 - c) * 64, 64)], skin, sk_sem, sibling, 5)
    left[slot_y, :] = total[...]
    sketch[:, pl.ds(pl.multiple_of(c * LANES, LANES), LANES)] = total[rows(c * 64, 64), :]

    for k in range(NY):
        ys = (y + k) % NY
        spot = part_of(c * NY + ys)
        if k > 0:
            landed(left.at[part_of(ys)], row_sem.at[ys])

        @pl.when(x == y)
        def _():
            right[spot, :] = left[part_of(ys), :]

        @pl.when(x != y)
        def _():
            landed(right.at[spot], col_sem.at[ys])

        send(right.at[spot], right.at[spot], fwd_sem.at[ys], sibling, 6)

    lhigh, llow = split(left[...])

    def product(h):
        rhigh, rlow = split(right[rows(h * (NY * SHARE), NY * SHARE), :])
        dims = (((0,), (0,)), ((), ()))
        out = lax.dot_general(lhigh, rhigh, dims, preferred_element_type=jnp.float32)
        out += lax.dot_general(lhigh, rlow, dims, preferred_element_type=jnp.float32)
        out += lax.dot_general(llow, rhigh, dims, preferred_element_type=jnp.float32)
        block[:, pl.ds(pl.multiple_of(h * LANES, LANES), LANES)] = out * (1.0 / 4096.0)

    product(c)
    landed(skin, sk_sem)
    sketch[:, pl.ds(pl.multiple_of((1 - c) * LANES, LANES), LANES)] = skin[...]
    for k in range(NY):
        landed(right.at[part_of((1 - c) * NY + k)], fwd_sem.at[k])
    product(1 - c)

    def strip(zz):
        return rows(zz * 16, 16)

    for p in range(NZ - 1):
        send(block.at[strip(z_of(p))], zgram.at[strip(p)], rs_sem.at[p], at_z(stride(p)), 7)
    acc = block[strip(z), :]
    for p in range(NZ - 2, -1, -1):
        landed(zgram.at[strip(p)], rs_sem.at[p])
        acc = acc + zgram[strip(p), :]

    def tile(cc, zz, yy, count):
        return gram.at[rows(cc * 128 + zz * 16, count), pl.ds(pl.multiple_of(yy * 256, 256), 256)]

    tile_mine = tile(c, z, y, 16)
    tile_mine[...] = acc
    send(tile_mine, tile_mine, yag_sem.at[2, z], at_y(2), 9)
    for p in range(NZ - 1):
        send(tile_mine, tile_mine, ag_sem.at[p], at_z(stride(p)), 8)

    def spread(zz):
        piece = tile(c, zz, y, 16)
        for k in (1, 3):
            send(piece, piece, yag_sem.at[k, zz], at_y(k), 9)

    def across(p):
        zz = (z - stride(p) + NZ) % NZ
        landed(tile(c, zz, y, 16), ag_sem.at[p])
        spread(zz)

    spread(z)
    across(6)
    across(5)
    opposite = (y + 2) % NY
    far = tile(c, z, opposite, 16)
    landed(far, yag_sem.at[2, z])
    for p in range(NZ - 1):
        send(far, far, far_sem.at[p], at_z(stride(p)), 13)
    for p in range(NZ - 4, -1, -1):
        across(p)

    def share(yy):
        whole = tile(c, 0, yy, 128)
        send(whole, whole, sib_sem.at[yy], sibling, 10)

    share(y)
    for k in (1, 3):
        ys = (y - k + NY) % NY
        for zz in range(NZ):
            landed(tile(c, zz, ys, 16), yag_sem.at[k, zz])
        share(ys)
    for p in range(NZ - 1):
        landed(tile(c, (z - stride(p) + NZ) % NZ, opposite, 16), far_sem.at[p])
    share(opposite)

    def left_here(ref, slot):
        pltpu.make_async_copy(ref, ref, send_sem.at[slot]).wait()

    left_here(table.at[pl.ds(0, CHIPS * SHARE)], 0)
    left_here(table.at[pl.ds(0, 3 * NZ * YROWS)], 1)
    left_here(table.at[pl.ds(0, (NZ - 1) * YROWS)], 2)
    left_here(table.at[pl.ds(0, 7 * NY * ZROWS)], 11)
    left_here(table.at[pl.ds(0, (NY - 1) * ZROWS)], 12)

    left_here(table.at[pl.ds(0, 3 * SHARE)], 3)
    left_here(table.at[pl.ds(0, 3 * SHARE)], 4)
    left_here(table.at[pl.ds(0, 64)], 5)
    left_here(table.at[pl.ds(0, 4 * SHARE)], 6)
    left_here(xbuf.at[pl.ds(0, 16 * (NZ - 1))], 7)
    left_here(xbuf.at[pl.ds(0, 16 * (NZ - 1))], 8)
    left_here(xbuf.at[pl.ds(0, 16 * (3 + 2 * (NZ - 1)))], 9)
    left_here(xbuf.at[pl.ds(0, 512)], 10)
    left_here(xbuf.at[pl.ds(0, 16 * (NZ - 1))], 13)
    for k in range(NY):
        landed(tile(1 - c, 0, k, 128), sib_sem.at[k])


def body(matrix, signs, samples):
    vmem = pltpu.VMEM
    f32 = jnp.float32
    dma = pltpu.SemaphoreType.DMA
    spec = pl.BlockSpec(memory_space=pltpu.VMEM)
    return pl.pallas_call(
        kernel,
        out_shape=(
            jax.ShapeDtypeStruct((64, 256), f32),
            jax.ShapeDtypeStruct((256, 1024), f32),
        ),
        in_specs=[pl.BlockSpec(memory_space=pltpu.HBM)] * 3,
        out_specs=(spec, spec),
        scratch_shapes=[
            vmem((BLOCK, 256), f32),
            vmem((BLOCK, 256), f32),
            vmem((4 * BLOCK, LANES), f32),
            vmem((CHIPS, SHARE), jnp.int32),
            vmem((CHIPS, SHARE), jnp.int32),
            vmem((CHIPS, SHARE), jnp.int32),
            pltpu.SMEM((CHIPS, SHARE), jnp.int32),
            vmem((CHIPS * YROWS, LANES), f32),
            vmem((CHIPS * YROWS, LANES), f32),
            vmem((CHIPS * YROWS, LANES), f32),
            vmem((CHIPS * ZROWS, LANES), f32),
            vmem((CHIPS * ZROWS, LANES), f32),
            vmem((CHIPS * ZROWS, LANES), f32),
            vmem((NY * NZ * YROWS, LANES), f32),
            vmem((NZ * YROWS, LANES), f32),
            vmem((7 * NY * ZROWS, LANES), f32),
            vmem((NY * ZROWS, LANES), f32),
            vmem((SHARE, LANES), f32),
            vmem((NY * SHARE, LANES), f32),
            vmem((2 * NY * SHARE, LANES), f32),
            vmem((64, LANES), f32),
            vmem((SHARE, 256), f32),
            vmem((SHARE, 256), f32),
            dma((BLOCK // CHUNK,)),
            dma((3,)),
            dma((CHIPS,)),
            dma((NZ,)),
            dma((NY, NZ)),
            dma((NZ,)),
            dma((7,)),
            dma((NY,)),
            dma,
            dma((NY,)),
            dma((NY,)),
            dma((NY,)),
            dma((NZ,)),
            dma((NZ,)),
            dma((NZ,)),
            dma((NY, NZ)),
            dma((NY,)),
            dma((14,)),
        ],
        compiler_params=pltpu.CompilerParams(
            collective_id=0, has_side_effects=True, vmem_limit_bytes=62 * 2**20
        ),
    )(matrix, signs.reshape(CHIPS, SHARE), samples.reshape(CHIPS, SHARE))


def solution(mesh):
    return jax.shard_map(
        body,
        mesh=mesh,
        in_specs=(P("row", "col"), P("row"), P()),
        out_specs=(P("row", "col"), P("col", None)),
        check_vma=False,
    )
```

```python
import jax
import jax.numpy as jnp
from jax import lax
from jax.experimental import pallas as pl
from jax.experimental.pallas import tpu as pltpu
from jax.sharding import PartitionSpec as P

MESH = pl.DeviceIdType.MESH
NX, NY, NZ = 4, 4, 8
CHIPS = NY * NZ
BLOCK = 4096
GROUP = 256
GROUPS = BLOCK // GROUP
SHARE = 128
LANES = 128
CHUNK = 512
YROWS = 88
ZROWS = SHARE - YROWS
FINISH = 4
SECOND_Z, THIRD_Z = 5, 9


def device(x, y, z, c):
    return (y * (NZ * 2) + z * 2 + c, x)


def parity(bits):
    bits = bits ^ (bits >> 4)
    bits = bits ^ (bits >> 2)
    bits = bits ^ (bits >> 1)
    return bits & 1


def stride(p):
    return (NZ - p) // 2 * (2 * (p % 2) - 1)


def split(values):
    high = values.astype(jnp.bfloat16)
    low = (values - high.astype(jnp.float32)).astype(jnp.bfloat16)
    return high, low


def rows(start, count):
    return pl.ds(pl.multiple_of(start, 8), count)


def kernel(
    matrix, whole_in, sketch, gram,
    xbuf, ybuf, table, signs, samples, picks, places,
    mine, other, theirs, minez, otherz, theirsz,
    ypart, zpart, zin, yin, total, left, right, skin, block, zgram,
    load_sem, place_sem, core_sem, corez_sem, ypart_sem, z_sem, zin_sem, yin_sem,
    sk_sem, row_sem, col_sem, fwd_sem, rs_sem, ag_sem, far_sem, yag_sem, sib_sem, send_sem,
):
    row = lax.axis_index("row")
    x = lax.axis_index("col")
    y, z, c = row // (NZ * 2), row // 2 % NZ, row % 2
    sibling = device(x, y, z, 1 - c)
    ahead = 1 - 2 * c

    def at_y(step):
        return device(x, (y + step + NY) % NY, z, c)

    def at_z(step):
        return device(x, y, (z + step + NZ) % NZ, c)

    def load(i):
        part = pl.ds(i * CHUNK, CHUNK)
        return pltpu.make_async_copy(matrix.at[part], xbuf.at[part], load_sem.at[i])

    def send(src, dst, sem, where, slot):
        pltpu.make_async_remote_copy(
            src, dst, send_sem.at[slot], sem, device_id=where, device_id_type=MESH
        ).start()

    def landed(ref, sem):
        pltpu.make_async_copy(ref, ref, sem).wait()

    barrier = pltpu.get_barrier_semaphore()

    def greet(where):
        pl.semaphore_signal(barrier, inc=1, device_id=where, device_id_type=MESH)

    get_signs = pltpu.make_async_copy(whole_in.at[pl.ds(CHIPS, CHIPS)], signs, place_sem.at[0])
    get_samples = pltpu.make_async_copy(whole_in.at[pl.ds(0, CHIPS)], samples, place_sem.at[1])
    get_samples.start()
    get_signs.start()
    for i in range(BLOCK // CHUNK):
        load(i).start()

    for p in range(NZ - 1):
        greet(at_z(stride(p)))
    for k in range(1, NY):
        greet(at_y(k))

    @pl.when(x != y)
    def _():
        for k in range(NY):
            greet(device(y, k, z, c))

    greet(sibling)

    get_samples.wait()
    spots = samples[...]
    flips = parity((spots // BLOCK) & row)
    picks[...] = spots % BLOCK + flips * (2 * BLOCK)
    place = pltpu.make_async_copy(picks, places, place_sem.at[2])
    place.start()

    line = lax.broadcasted_iota(jnp.int32, (GROUP, GROUP), 0)
    column = lax.broadcasted_iota(jnp.int32, (GROUP, GROUP), 1)
    hadamard = (1 - 2 * parity(line & column)).astype(jnp.float32) * (1.0 / 512.0)
    get_signs.wait()

    def mix(i, _):
        load(i).wait()
        for half in range(CHUNK // GROUP):
            g = i * (CHUNK // GROUP) + half
            sign = jnp.concatenate(
                [signs[pl.ds(2 * g, 1), :], signs[pl.ds(2 * g + 1, 1), :]], axis=1
            ).astype(jnp.float32)
            signed = (hadamard * sign).astype(jnp.bfloat16)
            part = rows(g * GROUP, GROUP)
            high, low = split(xbuf[part, :])
            ybuf[part, :] = jnp.dot(
                signed, high, preferred_element_type=jnp.float32
            ) + jnp.dot(signed, low, preferred_element_type=jnp.float32)
        return 0

    lax.fori_loop(0, BLOCK // CHUNK, mix, 0)

    def fold(t, _):
        for half in range(2):
            lanes = slice(half * LANES, (half + 1) * LANES)
            vals = [ybuf[rows(g * GROUP + t * 8, 8), lanes] for g in range(GROUPS)]
            step = 1
            while step < GROUPS:
                for g in range(GROUPS):
                    if g & step == 0:
                        a, b = vals[g], vals[g + step]
                        vals[g], vals[g + step] = a + b, a - b
                step *= 2
            place_of = jnp.where(c == half, 0, BLOCK)
            for g in range(GROUPS):
                spot = place_of + g * GROUP + t * 8
                table[rows(spot, 8), :] = vals[g]
                table[rows(spot + 2 * BLOCK, 8), :] = -vals[g]
        return 0

    lax.fori_loop(0, GROUP // 8, fold, 0)
    place.wait()

    def chunk(yy, zz):
        return yy * NZ + zz

    def gather(spot, first, count, kept_to, given_to, base):
        for start in range(0, count, 8):
            at = [places[spot, first + start + u] for u in range(8)]
            kept = [table[pl.ds(at[u], 1), :] for u in range(8)]
            given = [table[pl.ds(at[u] + BLOCK, 1), :] for u in range(8)]
            for u in range(8):
                kept_to[pl.ds(base + start + u, 1), :] = kept[u]
            for u in range(8):
                given_to[pl.ds(base + start + u, 1), :] = given[u]

    def part_y(spot):
        return rows(spot * YROWS, YROWS)

    def part_z(spot):
        return rows(spot * (NY * ZROWS), NY * ZROWS)

    def part_of(spot):
        return rows(spot * SHARE, SHARE)

    def y_of(q):
        return (y + 2 + q) % NY

    def z_of(p):
        return (z + stride(p) + NZ) % NZ

    def turn_z(step):
        return (z + step + NZ) % NZ

    def pick(p):
        def each(q, _):
            spot = chunk(y_of(q), z_of(p))
            gather(spot, 0, YROWS, mine, other, spot * YROWS)
            return 0

        lax.fori_loop(0, 4, each, 0)

    def give(p):
        def each(q, _):
            spot = chunk(y_of(q), z_of(p))
            send(other.at[part_y(spot)], theirs.at[part_y(spot)], core_sem.at[spot], sibling, 0)
            return 0

        lax.fori_loop(0, 4, each, 0)

    def merge(p):
        def each(q, _):
            spot = chunk(y_of(q), z_of(p))
            landed(theirs.at[part_y(spot)], core_sem.at[spot])
            mine[part_y(spot), :] += theirs[part_y(spot), :]
            return 0

        lax.fori_loop(0, 4, each, 0)
        for k in (2, 1, 3):
            spot = chunk((y + k) % NY, z_of(p))
            send(mine.at[part_y(spot)], ypart.at[part_y(k * NZ + p)], ypart_sem.at[k, p], at_y(k), 1)

    def finish(p):
        own = part_y(chunk(y, z_of(p)))
        for k in (1, 3, 2):
            landed(ypart.at[part_y(k * NZ + p)], ypart_sem.at[k, p])
        mine[own, :] += sum(ypart[part_y(k * NZ + p), :] for k in range(1, NY))

        @pl.when(p < NZ - 1)
        def _():
            send(mine.at[own], zpart.at[part_y(p)], z_sem.at[p], at_z(stride(p)), 2)

    def pick_z(p):
        zz = z_of(p)
        for yy in range(NY):
            gather(chunk(yy, zz), YROWS, ZROWS, minez, otherz, (zz * NY + yy) * ZROWS)
        send(otherz.at[part_z(zz)], theirsz.at[part_z(zz)], corez_sem.at[zz], sibling, 0)

    def send_z(zz, slot, hop):
        send(minez.at[part_z(zz)], zin.at[part_z(slot)], zin_sem.at[slot], at_z(hop), 11)

    def merge_z(p):
        zz = z_of(p)
        landed(theirsz.at[part_z(zz)], corez_sem.at[zz])
        minez[part_z(zz), :] += theirsz[part_z(zz), :]
        way = 2 * (p % 2) - 1
        hop = jnp.where(p == 0, 2 * ahead, way)
        slot = jnp.where(p == 0, 0, jnp.where(p < 3, 1, 3) + (1 - way * ahead) // 2)

        @pl.when(jnp.logical_or(p < 3, jnp.logical_or(p == 5, p == 6)))
        def _():
            send_z(zz, slot, hop)

    def take_z(step, slots):
        zz = turn_z(step)
        for slot in slots:
            landed(zin.at[part_z(slot)], zin_sem.at[slot])
        minez[part_z(zz), :] += sum(zin[part_z(slot), :] for slot in slots)

    def second_z():
        take_z(2 * ahead, (0, 1))
        send_z(turn_z(2 * ahead), 5, 2 * ahead)
        take_z(-2 * ahead, (2,))
        send_z(turn_z(-2 * ahead), 6, -2 * ahead)

    def third_z():
        take_z(0, (3, 4, 5, 6))
        for k in range(1, NY):
            part = rows((z * NY + (y + k) % NY) * ZROWS, ZROWS)
            slot = rows(k * ZROWS, ZROWS)
            send(minez.at[part], yin.at[slot], yin_sem.at[k], at_y(k), 12)

    pick(0)
    pl.semaphore_wait(barrier, NZ + NY + NX - 2)
    give(0)
    pick_z(0)
    pick(1)
    give(1)
    pick_z(1)

    def turn(t, _):
        @pl.when(t < NZ)
        def _():
            merge(t)
            merge_z(t)

        @pl.when(t < NZ - 2)
        def _():
            pick(t + 2)
            give(t + 2)
            pick_z(t + 2)

        @pl.when(t == SECOND_Z)
        def _():
            second_z()

        @pl.when(t == THIRD_Z)
        def _():
            third_z()

        @pl.when(t >= FINISH)
        def _():
            finish(t - FINISH)

        return 0

    lax.fori_loop(0, NZ + FINISH, turn, 0)

    home = part_y(chunk(y, z))
    for k in range(1, NY):
        landed(yin.at[rows(k * ZROWS, ZROWS)], yin_sem.at[k])
    total[pl.ds(YROWS, ZROWS), :] = minez[rows((z * NY + y) * ZROWS, ZROWS), :] + sum(
        yin[rows(k * ZROWS, ZROWS), :] for k in range(1, NY)
    )
    for p in range(NZ - 1):
        landed(zpart.at[part_y(p)], z_sem.at[p])
    total[pl.ds(0, YROWS), :] = mine[home, :] + sum(zpart[part_y(p), :] for p in range(NZ - 1))

    slot_y = part_of(y)
    slot_cy = part_of(c * NY + y)
    for j in (2, 1, 3):
        send(total, right.at[slot_cy], col_sem.at[y], device((x + j) % NX, x, z, c), 3)
    for k in (2, 1, 3):
        send(total, left.at[slot_y], row_sem.at[y], at_y(k), 4)
    send(total.at[rows((1 - c) * 64, 64)], skin, sk_sem, sibling, 5)
    left[slot_y, :] = total[...]
    sketch[:, pl.ds(pl.multiple_of(c * LANES, LANES), LANES)] = total[rows(c * 64, 64), :]

    for k in range(NY):
        ys = (y + k) % NY
        spot = part_of(c * NY + ys)
        if k > 0:
            landed(left.at[part_of(ys)], row_sem.at[ys])

        @pl.when(x == y)
        def _():
            right[spot, :] = left[part_of(ys), :]

        @pl.when(x != y)
        def _():
            landed(right.at[spot], col_sem.at[ys])

        send(right.at[spot], right.at[spot], fwd_sem.at[ys], sibling, 6)

    lhigh, llow = split(left[...])

    def product(h):
        rhigh, rlow = split(right[rows(h * (NY * SHARE), NY * SHARE), :])
        dims = (((0,), (0,)), ((), ()))
        out = lax.dot_general(lhigh, rhigh, dims, preferred_element_type=jnp.float32)
        out += lax.dot_general(lhigh, rlow, dims, preferred_element_type=jnp.float32)
        out += lax.dot_general(llow, rhigh, dims, preferred_element_type=jnp.float32)
        block[:, pl.ds(pl.multiple_of(h * LANES, LANES), LANES)] = out * (1.0 / 4096.0)

    def strip(zz):
        return rows(zz * 16, 16)

    def pass_on(h, turn):
        lanes = pl.ds(pl.multiple_of(h * LANES, LANES), LANES)
        for p in range(NZ - 1):
            send(
                block.at[strip(z_of(p)), lanes], zgram.at[strip(p), lanes],
                rs_sem.at[turn, p], at_z(stride(p)), 7,
            )

    product(c)
    pass_on(c, 0)
    landed(skin, sk_sem)
    sketch[:, pl.ds(pl.multiple_of((1 - c) * LANES, LANES), LANES)] = skin[...]
    for k in range(NY):
        landed(right.at[part_of((1 - c) * NY + k)], fwd_sem.at[k])
    product(1 - c)
    pass_on(1 - c, 1)

    acc = block[strip(z), :]
    for p in range(NZ - 2, -1, -1):
        landed(zgram.at[strip(p), pl.ds(0, LANES)], rs_sem.at[0, p])
        landed(zgram.at[strip(p), pl.ds(0, LANES)], rs_sem.at[1, p])
        acc = acc + zgram[strip(p), :]

    def tile(cc, zz, yy, count):
        return gram.at[rows(cc * 128 + zz * 16, count), pl.ds(pl.multiple_of(yy * 256, 256), 256)]

    tile_mine = tile(c, z, y, 16)
    tile_mine[...] = acc
    send(tile_mine, tile_mine, yag_sem.at[2, z], at_y(2), 9)
    for p in range(NZ - 1):
        send(tile_mine, tile_mine, ag_sem.at[p], at_z(stride(p)), 8)

    def spread(zz):
        piece = tile(c, zz, y, 16)
        for k in (1, 3):
            send(piece, piece, yag_sem.at[k, zz], at_y(k), 9)

    def across(p):
        zz = (z - stride(p) + NZ) % NZ
        landed(tile(c, zz, y, 16), ag_sem.at[p])
        spread(zz)

    spread(z)
    across(6)
    across(5)
    opposite = (y + 2) % NY
    far = tile(c, z, opposite, 16)
    landed(far, yag_sem.at[2, z])
    for p in range(NZ - 1):
        send(far, far, far_sem.at[p], at_z(stride(p)), 13)
    for p in range(NZ - 4, -1, -1):
        across(p)

    def share(yy):
        whole = tile(c, 0, yy, 128)
        send(whole, whole, sib_sem.at[yy], sibling, 10)

    share(y)
    for k in (1, 3):
        ys = (y - k + NY) % NY
        for zz in range(NZ):
            landed(tile(c, zz, ys, 16), yag_sem.at[k, zz])
        share(ys)
    for p in range(NZ - 1):
        landed(tile(c, (z - stride(p) + NZ) % NZ, opposite, 16), far_sem.at[p])
    share(opposite)

    def left_here(ref, slot):
        pltpu.make_async_copy(ref, ref, send_sem.at[slot]).wait()

    left_here(table.at[pl.ds(0, CHIPS * SHARE)], 0)
    left_here(table.at[pl.ds(0, 3 * NZ * YROWS)], 1)
    left_here(table.at[pl.ds(0, (NZ - 1) * YROWS)], 2)
    left_here(table.at[pl.ds(0, 7 * NY * ZROWS)], 11)
    left_here(table.at[pl.ds(0, (NY - 1) * ZROWS)], 12)

    left_here(table.at[pl.ds(0, 3 * SHARE)], 3)
    left_here(table.at[pl.ds(0, 3 * SHARE)], 4)
    left_here(table.at[pl.ds(0, 64)], 5)
    left_here(table.at[pl.ds(0, 4 * SHARE)], 6)
    left_here(xbuf.at[pl.ds(0, 16 * (NZ - 1))], 7)
    left_here(xbuf.at[pl.ds(0, 16 * (NZ - 1))], 8)
    left_here(xbuf.at[pl.ds(0, 16 * (3 + 2 * (NZ - 1)))], 9)
    left_here(xbuf.at[pl.ds(0, 512)], 10)
    left_here(xbuf.at[pl.ds(0, 16 * (NZ - 1))], 13)
    for k in range(NY):
        landed(tile(1 - c, 0, k, 128), sib_sem.at[k])


def body(matrix, signs, samples):
    vmem = pltpu.VMEM
    f32 = jnp.float32
    dma = pltpu.SemaphoreType.DMA
    spec = pl.BlockSpec(memory_space=pltpu.VMEM)
    return pl.pallas_call(
        kernel,
        out_shape=(
            jax.ShapeDtypeStruct((64, 256), f32),
            jax.ShapeDtypeStruct((256, 1024), f32),
        ),
        in_specs=[pl.BlockSpec(memory_space=pltpu.HBM)] * 2,
        out_specs=(spec, spec),
        scratch_shapes=[
            vmem((BLOCK, 256), f32),
            vmem((BLOCK, 256), f32),
            vmem((4 * BLOCK, LANES), f32),
            vmem((CHIPS, SHARE), jnp.int32),
            vmem((CHIPS, SHARE), jnp.int32),
            vmem((CHIPS, SHARE), jnp.int32),
            pltpu.SMEM((CHIPS, SHARE), jnp.int32),
            vmem((CHIPS * YROWS, LANES), f32),
            vmem((CHIPS * YROWS, LANES), f32),
            vmem((CHIPS * YROWS, LANES), f32),
            vmem((CHIPS * ZROWS, LANES), f32),
            vmem((CHIPS * ZROWS, LANES), f32),
            vmem((CHIPS * ZROWS, LANES), f32),
            vmem((NY * NZ * YROWS, LANES), f32),
            vmem((NZ * YROWS, LANES), f32),
            vmem((7 * NY * ZROWS, LANES), f32),
            vmem((NY * ZROWS, LANES), f32),
            vmem((SHARE, LANES), f32),
            vmem((NY * SHARE, LANES), f32),
            vmem((2 * NY * SHARE, LANES), f32),
            vmem((64, LANES), f32),
            vmem((SHARE, 256), f32),
            vmem((SHARE, 256), f32),
            dma((BLOCK // CHUNK,)),
            dma((3,)),
            dma((CHIPS,)),
            dma((NZ,)),
            dma((NY, NZ)),
            dma((NZ,)),
            dma((7,)),
            dma((NY,)),
            dma,
            dma((NY,)),
            dma((NY,)),
            dma((NY,)),
            dma((2, NZ)),
            dma((NZ,)),
            dma((NZ,)),
            dma((NY, NZ)),
            dma((NY,)),
            dma((14,)),
        ],
        compiler_params=pltpu.CompilerParams(
            collective_id=0, has_side_effects=True, vmem_limit_bytes=52 * 2**20
        ),
    )(matrix, jnp.concatenate([samples, signs]).reshape(2 * CHIPS, SHARE))


def solution(mesh):
    return jax.shard_map(
        body,
        mesh=mesh,
        in_specs=(P("row", "col"), P("row"), P()),
        out_specs=(P("row", "col"), P("col", None)),
        check_vma=False,
    )
```

```python
import jax
import jax.numpy as jnp
from jax import lax
from jax.experimental import pallas as pl
from jax.experimental.pallas import tpu as pltpu
from jax.sharding import PartitionSpec as P

MESH = pl.DeviceIdType.MESH
NX, NY, NZ = 4, 4, 8
CHIPS = NY * NZ
BLOCK = 4096
GROUP = 256
GROUPS = BLOCK // GROUP
SHARE = 128
LANES = 128
CHUNK = 512
YROWS = 88
ZROWS = SHARE - YROWS
FINISH = 4
SECOND_Z, THIRD_Z = 5, 9


def device(x, y, z, c):
    return (y * (NZ * 2) + z * 2 + c, x)


def parity(bits):
    bits = bits ^ (bits >> 4)
    bits = bits ^ (bits >> 2)
    bits = bits ^ (bits >> 1)
    return bits & 1


def stride(p):
    return (NZ - p) // 2 * (2 * (p % 2) - 1)


def split(values):
    high = values.astype(jnp.bfloat16)
    low = (values - high.astype(jnp.float32)).astype(jnp.bfloat16)
    return high, low


def rows(start, count):
    return pl.ds(pl.multiple_of(start, 8), count)


def kernel(
    matrix, whole_in, sketch, gram,
    xbuf, ybuf, table, signs, samples, picks, places,
    mine, other, theirs, minez, otherz, theirsz,
    ypart, zpart, zin, yin, total, left, right, skin, block, zgram,
    load_sem, place_sem, core_sem, corez_sem, ypart_sem, z_sem, zin_sem, yin_sem,
    sk_sem, row_sem, col_sem, fwd_sem, rs_sem, ag_sem, far_sem, yag_sem, sib_sem, send_sem,
):
    row = lax.axis_index("row")
    x = lax.axis_index("col")
    y, z, c = row // (NZ * 2), row // 2 % NZ, row % 2
    sibling = device(x, y, z, 1 - c)
    ahead = 1 - 2 * c

    def at_y(step):
        return device(x, (y + step + NY) % NY, z, c)

    def at_z(step):
        return device(x, y, (z + step + NZ) % NZ, c)

    def load(i):
        part = pl.ds(i * CHUNK, CHUNK)
        return pltpu.make_async_copy(matrix.at[part], xbuf.at[part], load_sem.at[i])

    def send(src, dst, sem, where, slot):
        pltpu.make_async_remote_copy(
            src, dst, send_sem.at[slot], sem, device_id=where, device_id_type=MESH
        ).start()

    def landed(ref, sem):
        pltpu.make_async_copy(ref, ref, sem).wait()

    barrier = pltpu.get_barrier_semaphore()

    def greet(where):
        pl.semaphore_signal(barrier, inc=1, device_id=where, device_id_type=MESH)

    get_signs = pltpu.make_async_copy(whole_in.at[pl.ds(CHIPS, CHIPS)], signs, place_sem.at[0])
    get_samples = pltpu.make_async_copy(whole_in.at[pl.ds(0, CHIPS)], samples, place_sem.at[1])
    get_samples.start()
    get_signs.start()
    for i in range(BLOCK // CHUNK):
        load(i).start()

    for p in range(NZ - 1):
        greet(at_z(stride(p)))
    for k in range(1, NY):
        greet(at_y(k))

    @pl.when(x != y)
    def _():
        for k in range(NY):
            greet(device(y, k, z, c))

    greet(sibling)

    get_samples.wait()
    spots = samples[...]
    flips = parity((spots // BLOCK) & row)
    picks[...] = spots % BLOCK + flips * (2 * BLOCK)
    place = pltpu.make_async_copy(picks, places, place_sem.at[2])
    place.start()

    line = lax.broadcasted_iota(jnp.int32, (GROUP, GROUP), 0)
    column = lax.broadcasted_iota(jnp.int32, (GROUP, GROUP), 1)
    hadamard = (1 - 2 * parity(line & column)).astype(jnp.float32) * (1.0 / 512.0)
    get_signs.wait()

    def mix(i, _):
        load(i).wait()
        for half in range(CHUNK // GROUP):
            g = i * (CHUNK // GROUP) + half
            sign = jnp.concatenate(
                [signs[pl.ds(2 * g, 1), :], signs[pl.ds(2 * g + 1, 1), :]], axis=1
            ).astype(jnp.float32)
            signed = (hadamard * sign).astype(jnp.bfloat16)
            part = rows(g * GROUP, GROUP)
            high, low = split(xbuf[part, :])
            ybuf[part, :] = jnp.dot(
                signed, high, preferred_element_type=jnp.float32
            ) + jnp.dot(signed, low, preferred_element_type=jnp.float32)
        return 0

    lax.fori_loop(0, BLOCK // CHUNK, mix, 0)

    def fold(t, _):
        for half in range(2):
            lanes = slice(half * LANES, (half + 1) * LANES)
            vals = [ybuf[rows(g * GROUP + t * 8, 8), lanes] for g in range(GROUPS)]
            step = 1
            while step < GROUPS:
                for g in range(GROUPS):
                    if g & step == 0:
                        a, b = vals[g], vals[g + step]
                        vals[g], vals[g + step] = a + b, a - b
                step *= 2
            place_of = jnp.where(c == half, 0, BLOCK)
            for g in range(GROUPS):
                spot = place_of + g * GROUP + t * 8
                table[rows(spot, 8), :] = vals[g]
                table[rows(spot + 2 * BLOCK, 8), :] = -vals[g]
        return 0

    lax.fori_loop(0, GROUP // 8, fold, 0)
    place.wait()

    def chunk(yy, zz):
        return yy * NZ + zz

    def gather(spot, first, count, kept_to, given_to, base):
        for start in range(0, count, 8):
            at = [places[spot, first + start + u] for u in range(8)]
            kept = [table[pl.ds(at[u], 1), :] for u in range(8)]
            given = [table[pl.ds(at[u] + BLOCK, 1), :] for u in range(8)]
            for u in range(8):
                kept_to[pl.ds(base + start + u, 1), :] = kept[u]
            for u in range(8):
                given_to[pl.ds(base + start + u, 1), :] = given[u]

    def part_y(spot):
        return rows(spot * YROWS, YROWS)

    def part_z(spot):
        return rows(spot * (NY * ZROWS), NY * ZROWS)

    def part_of(spot):
        return rows(spot * SHARE, SHARE)

    def y_of(q):
        return (y + 2 + q) % NY

    def z_of(p):
        return (z + stride(p) + NZ) % NZ

    def turn_z(step):
        return (z + step + NZ) % NZ

    def pick(p):
        def each(q, _):
            spot = chunk(y_of(q), z_of(p))
            gather(spot, 0, YROWS, mine, other, spot * YROWS)
            return 0

        lax.fori_loop(0, 4, each, 0)

    def give(p):
        def each(q, _):
            spot = chunk(y_of(q), z_of(p))
            send(other.at[part_y(spot)], theirs.at[part_y(spot)], core_sem.at[spot], sibling, 0)
            return 0

        lax.fori_loop(0, 4, each, 0)

    def merge(p):
        def each(q, _):
            spot = chunk(y_of(q), z_of(p))
            landed(theirs.at[part_y(spot)], core_sem.at[spot])
            mine[part_y(spot), :] += theirs[part_y(spot), :]
            k = (2 + q) % NY

            @pl.when(k != 0)
            def _():
                slot = k * NZ + p
                send(mine.at[part_y(spot)], ypart.at[part_y(slot)], ypart_sem.at[k, p], at_y(k), 1)

            return 0

        lax.fori_loop(0, 4, each, 0)

    def finish(p):
        own = part_y(chunk(y, z_of(p)))
        for k in (1, 3, 2):
            landed(ypart.at[part_y(k * NZ + p)], ypart_sem.at[k, p])
        mine[own, :] += sum(ypart[part_y(k * NZ + p), :] for k in range(1, NY))

        @pl.when(p < NZ - 1)
        def _():
            send(mine.at[own], zpart.at[part_y(p)], z_sem.at[p], at_z(stride(p)), 2)

    def pick_z(p):
        zz = z_of(p)
        for yy in range(NY):
            gather(chunk(yy, zz), YROWS, ZROWS, minez, otherz, (zz * NY + yy) * ZROWS)
        send(otherz.at[part_z(zz)], theirsz.at[part_z(zz)], corez_sem.at[zz], sibling, 0)

    def send_z(zz, slot, hop):
        send(minez.at[part_z(zz)], zin.at[part_z(slot)], zin_sem.at[slot], at_z(hop), 11)

    def merge_z(p):
        zz = z_of(p)
        landed(theirsz.at[part_z(zz)], corez_sem.at[zz])
        minez[part_z(zz), :] += theirsz[part_z(zz), :]
        way = 2 * (p % 2) - 1
        hop = jnp.where(p == 0, 2 * ahead, way)
        slot = jnp.where(p == 0, 0, jnp.where(p < 3, 1, 3) + (1 - way * ahead) // 2)

        @pl.when(jnp.logical_or(p < 3, jnp.logical_or(p == 5, p == 6)))
        def _():
            send_z(zz, slot, hop)

    def take_z(step, slots):
        zz = turn_z(step)
        for slot in slots:
            landed(zin.at[part_z(slot)], zin_sem.at[slot])
        minez[part_z(zz), :] += sum(zin[part_z(slot), :] for slot in slots)

    def second_z():
        take_z(2 * ahead, (0, 1))
        send_z(turn_z(2 * ahead), 5, 2 * ahead)
        take_z(-2 * ahead, (2,))
        send_z(turn_z(-2 * ahead), 6, -2 * ahead)

    def third_z():
        take_z(0, (3, 4, 5, 6))
        for k in range(1, NY):
            part = rows((z * NY + (y + k) % NY) * ZROWS, ZROWS)
            slot = rows(k * ZROWS, ZROWS)
            send(minez.at[part], yin.at[slot], yin_sem.at[k], at_y(k), 12)

    pick(0)
    pl.semaphore_wait(barrier, NZ + NY + NX - 2)
    give(0)
    pick_z(0)
    pick_z(1)

    def turn(t, _):
        @pl.when(t < NZ)
        def _():
            merge(t)
            merge_z(t)

        @pl.when(t == 0)
        def _():
            pick(1)
            give(1)

        @pl.when(t < NZ - 2)
        def _():
            pick(t + 2)
            give(t + 2)
            pick_z(t + 2)

        @pl.when(t == SECOND_Z)
        def _():
            second_z()

        @pl.when(t == THIRD_Z)
        def _():
            third_z()

        @pl.when(t >= FINISH)
        def _():
            finish(t - FINISH)

        return 0

    lax.fori_loop(0, NZ + FINISH, turn, 0)

    home = part_y(chunk(y, z))
    for k in range(1, NY):
        landed(yin.at[rows(k * ZROWS, ZROWS)], yin_sem.at[k])
    total[pl.ds(YROWS, ZROWS), :] = minez[rows((z * NY + y) * ZROWS, ZROWS), :] + sum(
        yin[rows(k * ZROWS, ZROWS), :] for k in range(1, NY)
    )
    for p in range(NZ - 1):
        landed(zpart.at[part_y(p)], z_sem.at[p])
    total[pl.ds(0, YROWS), :] = mine[home, :] + sum(zpart[part_y(p), :] for p in range(NZ - 1))

    slot_y = part_of(y)
    slot_cy = part_of(c * NY + y)
    for j in (2, 1, 3):
        send(total, right.at[slot_cy], col_sem.at[y], device((x + j) % NX, x, z, c), 3)
    for k in (2, 1, 3):
        send(total, left.at[slot_y], row_sem.at[y], at_y(k), 4)
    send(total.at[rows((1 - c) * 64, 64)], skin, sk_sem, sibling, 5)
    left[slot_y, :] = total[...]
    sketch[:, pl.ds(pl.multiple_of(c * LANES, LANES), LANES)] = total[rows(c * 64, 64), :]

    for k in range(NY):
        ys = (y + k) % NY
        spot = part_of(c * NY + ys)
        if k > 0:
            landed(left.at[part_of(ys)], row_sem.at[ys])

        @pl.when(x == y)
        def _():
            right[spot, :] = left[part_of(ys), :]

        @pl.when(x != y)
        def _():
            landed(right.at[spot], col_sem.at[ys])

        send(right.at[spot], right.at[spot], fwd_sem.at[ys], sibling, 6)

    lhigh, llow = split(left[...])

    def product(h):
        rhigh, rlow = split(right[rows(h * (NY * SHARE), NY * SHARE), :])
        dims = (((0,), (0,)), ((), ()))
        out = lax.dot_general(lhigh, rhigh, dims, preferred_element_type=jnp.float32)
        out += lax.dot_general(lhigh, rlow, dims, preferred_element_type=jnp.float32)
        out += lax.dot_general(llow, rhigh, dims, preferred_element_type=jnp.float32)
        block[:, pl.ds(pl.multiple_of(h * LANES, LANES), LANES)] = out * (1.0 / 4096.0)

    def strip(zz):
        return rows(zz * 16, 16)

    def pass_on(h, turn):
        lanes = pl.ds(pl.multiple_of(h * LANES, LANES), LANES)
        for p in range(NZ - 1):
            send(
                block.at[strip(z_of(p)), lanes], zgram.at[strip(p), lanes],
                rs_sem.at[turn, p], at_z(stride(p)), 7,
            )

    product(c)
    pass_on(c, 0)
    landed(skin, sk_sem)
    sketch[:, pl.ds(pl.multiple_of((1 - c) * LANES, LANES), LANES)] = skin[...]
    for k in range(NY):
        landed(right.at[part_of((1 - c) * NY + k)], fwd_sem.at[k])
    product(1 - c)
    pass_on(1 - c, 1)

    acc = block[strip(z), :]
    for p in range(NZ - 2, -1, -1):
        landed(zgram.at[strip(p), pl.ds(0, LANES)], rs_sem.at[0, p])
        landed(zgram.at[strip(p), pl.ds(0, LANES)], rs_sem.at[1, p])
        acc = acc + zgram[strip(p), :]

    def tile(cc, zz, yy, count):
        return gram.at[rows(cc * 128 + zz * 16, count), pl.ds(pl.multiple_of(yy * 256, 256), 256)]

    tile_mine = tile(c, z, y, 16)
    tile_mine[...] = acc
    send(tile_mine, tile_mine, yag_sem.at[2, z], at_y(2), 9)
    for p in range(NZ - 1):
        send(tile_mine, tile_mine, ag_sem.at[p], at_z(stride(p)), 8)

    def spread(zz):
        piece = tile(c, zz, y, 16)
        for k in (1, 3):
            send(piece, piece, yag_sem.at[k, zz], at_y(k), 9)

    def across(p):
        zz = (z - stride(p) + NZ) % NZ
        landed(tile(c, zz, y, 16), ag_sem.at[p])
        spread(zz)

    spread(z)
    across(6)
    across(5)
    opposite = (y + 2) % NY
    far = tile(c, z, opposite, 16)
    landed(far, yag_sem.at[2, z])
    for p in range(NZ - 1):
        send(far, far, far_sem.at[p], at_z(stride(p)), 13)
    for p in range(NZ - 4, -1, -1):
        across(p)

    def share(yy):
        whole = tile(c, 0, yy, 128)
        send(whole, whole, sib_sem.at[yy], sibling, 10)

    share(y)
    for k in (1, 3):
        ys = (y - k + NY) % NY
        for zz in range(NZ):
            landed(tile(c, zz, ys, 16), yag_sem.at[k, zz])
        share(ys)
    for p in range(NZ - 1):
        landed(tile(c, (z - stride(p) + NZ) % NZ, opposite, 16), far_sem.at[p])
    share(opposite)

    def left_here(ref, slot):
        pltpu.make_async_copy(ref, ref, send_sem.at[slot]).wait()

    left_here(table.at[pl.ds(0, CHIPS * SHARE)], 0)
    left_here(table.at[pl.ds(0, 3 * NZ * YROWS)], 1)
    left_here(table.at[pl.ds(0, (NZ - 1) * YROWS)], 2)
    left_here(table.at[pl.ds(0, 7 * NY * ZROWS)], 11)
    left_here(table.at[pl.ds(0, (NY - 1) * ZROWS)], 12)

    left_here(table.at[pl.ds(0, 3 * SHARE)], 3)
    left_here(table.at[pl.ds(0, 3 * SHARE)], 4)
    left_here(table.at[pl.ds(0, 64)], 5)
    left_here(table.at[pl.ds(0, 4 * SHARE)], 6)
    left_here(xbuf.at[pl.ds(0, 16 * (NZ - 1))], 7)
    left_here(xbuf.at[pl.ds(0, 16 * (NZ - 1))], 8)
    left_here(xbuf.at[pl.ds(0, 16 * (3 + 2 * (NZ - 1)))], 9)
    left_here(xbuf.at[pl.ds(0, 512)], 10)
    left_here(xbuf.at[pl.ds(0, 16 * (NZ - 1))], 13)
    for k in range(NY):
        landed(tile(1 - c, 0, k, 128), sib_sem.at[k])


def body(matrix, signs, samples):
    vmem = pltpu.VMEM
    f32 = jnp.float32
    dma = pltpu.SemaphoreType.DMA
    spec = pl.BlockSpec(memory_space=pltpu.VMEM)
    return pl.pallas_call(
        kernel,
        out_shape=(
            jax.ShapeDtypeStruct((64, 256), f32),
            jax.ShapeDtypeStruct((256, 1024), f32),
        ),
        in_specs=[pl.BlockSpec(memory_space=pltpu.HBM)] * 2,
        out_specs=(spec, spec),
        scratch_shapes=[
            vmem((BLOCK, 256), f32),
            vmem((BLOCK, 256), f32),
            vmem((4 * BLOCK, LANES), f32),
            vmem((CHIPS, SHARE), jnp.int32),
            vmem((CHIPS, SHARE), jnp.int32),
            vmem((CHIPS, SHARE), jnp.int32),
            pltpu.SMEM((CHIPS, SHARE), jnp.int32),
            vmem((CHIPS * YROWS, LANES), f32),
            vmem((CHIPS * YROWS, LANES), f32),
            vmem((CHIPS * YROWS, LANES), f32),
            vmem((CHIPS * ZROWS, LANES), f32),
            vmem((CHIPS * ZROWS, LANES), f32),
            vmem((CHIPS * ZROWS, LANES), f32),
            vmem((NY * NZ * YROWS, LANES), f32),
            vmem((NZ * YROWS, LANES), f32),
            vmem((7 * NY * ZROWS, LANES), f32),
            vmem((NY * ZROWS, LANES), f32),
            vmem((SHARE, LANES), f32),
            vmem((NY * SHARE, LANES), f32),
            vmem((2 * NY * SHARE, LANES), f32),
            vmem((64, LANES), f32),
            vmem((SHARE, 256), f32),
            vmem((SHARE, 256), f32),
            dma((BLOCK // CHUNK,)),
            dma((3,)),
            dma((CHIPS,)),
            dma((NZ,)),
            dma((NY, NZ)),
            dma((NZ,)),
            dma((7,)),
            dma((NY,)),
            dma,
            dma((NY,)),
            dma((NY,)),
            dma((NY,)),
            dma((2, NZ)),
            dma((NZ,)),
            dma((NZ,)),
            dma((NY, NZ)),
            dma((NY,)),
            dma((14,)),
        ],
        compiler_params=pltpu.CompilerParams(
            collective_id=0, has_side_effects=True, vmem_limit_bytes=52 * 2**20
        ),
    )(matrix, jnp.concatenate([samples, signs]).reshape(2 * CHIPS, SHARE))


def solution(mesh):
    return jax.shard_map(
        body,
        mesh=mesh,
        in_specs=(P("row", "col"), P("row"), P()),
        out_specs=(P("row", "col"), P("col", None)),
        check_vma=False,
    )
```
